128 devices in a mesh: dp: 8 (over x, core), mp: 16 (over y, z).
Axes of the slice: x: 4, y: 4, z: 4, core: 2. Of those that a mesh axis runs over, the one named last changes fastest.
Arguments:
- features: bfloat16 [131072, 1024], P('dp', 'mp'), may hold values from -6 to 6
- weights1: bfloat16 [1024, 1024], P('mp'), may hold values from -0.1875 to 0.1875
- bias1: float32 [512], replicated, may hold values from -3 to 3
- weights2: bfloat16 [512, 1024], replicated, may hold values from -0.25 to 0.25
- bias2: float32 [512], replicated, may hold values from -3 to 3
- send_rows: int32 [128, 128, 8], P(('dp', 'mp')), may hold values from 0 to 1023
- tile_dst: int32 [128, 128], P(('dp', 'mp')), may hold values from 0 to 7
- tile_src: int32 [128, 128], P(('dp', 'mp')), may hold values from 0 to 15
- tile_count: int32 [128], P(('dp', 'mp')), may hold values from 32 to 128, as said below
- tile_vals: bfloat16 [128, 128, 128, 128], P(('dp', 'mp')), may hold values from 0 to 0.001953125
Outputs:
- embedded: bfloat16 [131072, 512], P(('dp', 'mp'))
The draws below stay inside these ranges and needn't reach their ends.
Inputs may be any that keep to these rules, and one draw needn't show every extreme that they name: `tile_count`: each partition's slots name distinct pairs of row tile and source tile; one partition has all 128 slots live.
All inputs are finite; a program needn't handle non-finite values.
Results may differ from the reference program's by a relative error of at most 0.004.
Values may be sent and summed in bfloat16 or wider, within the bound.
A program may use at most 192 MiB of HBM per device.

```python
import jax
import jax.numpy as jnp
from jax import lax

F = 1024
HID = 512
ND = 1024
TILE = 128
H = 8
NODES = 131072
SRC_TILES = 16
PAIRS = 128
DEVICES = 128


def tile_pairs(key):
    keys = jax.random.split(key, DEVICES)
    return jax.vmap(lambda one_key: jax.random.permutation(one_key, PAIRS))(keys).astype(jnp.int32)


def draw_tile_dst(key, part):
    return (tile_pairs(key) // SRC_TILES).astype(jnp.int32)


def draw_tile_src(key, part):
    return (tile_pairs(key) % SRC_TILES).astype(jnp.int32)


def draw_tile_count(key, part):
    key = jax.random.fold_in(key, 5)
    first_key, second_key = jax.random.split(key)
    counts = jax.random.randint(first_key, (DEVICES,), PAIRS // 4, PAIRS + 1)
    fullest = jax.random.randint(second_key, (), 0, DEVICES)
    return jnp.where(jnp.arange(DEVICES) == fullest, PAIRS, counts).astype(jnp.int32)


def with_ends(entries, stream_key, least, high):
    longest = entries.shape.index(max(entries.shape))
    spots = []
    for shift in (0, 1):
        where = [jax.random.randint(jax.random.fold_in(stream_key, axis), (), 0, length) for axis, length in enumerate(entries.shape)]
        where[longest] = (where[longest] + shift) % entries.shape[longest]
        spots.append(tuple(where))
    return entries.at[spots[0]].set(least).at[spots[1]].set(high)


def levels(rng, dims, shards, low, top_value):
    gain, own = 1.0, jax.random.fold_in(rng, 6)
    for axis_at, parts in shards:
        draws = jnp.exp(jax.random.uniform(jax.random.fold_in(own, axis_at), (parts,), jnp.float32, low / len(shards), top_value / len(shards)))
        gain = gain * jnp.repeat(draws, dims[axis_at] // parts).reshape([-1 if axis == axis_at else 1 for axis in range(len(dims))])
    return gain


def scatter_about(rng, dims, spread, reach, cuts=(), kind=jnp.bfloat16):
    level = levels(rng, dims, cuts, -0.22, 0.18) if cuts else 1.0
    entries = jax.random.normal(rng, dims, jnp.float32) * spread * level
    return jnp.minimum(jnp.maximum(entries, -reach), reach).astype(kind)


def setup_inputs(seed: int = 0) -> dict:
    splits = jax.random.split(jax.random.key(seed), 11)
    return {
        "features": scatter_about(splits[0], (NODES, F), 1.0, 6.0, ((0, 8), (1, 16))),
        "weights1": scatter_about(splits[1], (F, 2 * HID), F ** -0.5, 0.1875, ((0, 16),)),
        "bias1": scatter_about(splits[2], (HID,), 0.5, 3.0, (), jnp.float32),
        "weights2": scatter_about(splits[3], (HID, 2 * HID), HID ** -0.5, 0.25),
        "bias2": scatter_about(splits[4], (HID,), 0.5, 3.0, (), jnp.float32),
        "send_rows": with_ends(jax.random.randint(splits[5], (DEVICES, DEVICES, H), 0, ND), jax.random.fold_in(splits[5], 1), 0, ND - 1).astype(jnp.int32),
        "tile_dst": draw_tile_dst(jax.random.fold_in(splits[10], 71), 0),
        "tile_src": draw_tile_src(jax.random.fold_in(splits[10], 71), 0),
        "tile_count": draw_tile_count(jax.random.fold_in(splits[10], 71), 0),
        "tile_vals": jnp.clip(0.001953125 * jax.random.uniform(splits[9], (DEVICES, PAIRS, TILE, TILE), jnp.float32) ** levels(splits[9], (DEVICES, PAIRS, TILE, TILE), ((0, 128),), -0.2, 0.2), 0.0, 0.001953125).astype(jnp.bfloat16),
    }


def aggregate(vals, dst, src, count, source):
    live = (jnp.arange(vals.shape[0], dtype=jnp.int32) < count).astype(jnp.float32)
    dense = jnp.zeros((ND // TILE, SRC_TILES, TILE, TILE), jnp.float32)
    dense = dense.at[dst, src].add(vals.astype(jnp.float32) * live[:, None, None])
    dense = dense.transpose(0, 2, 1, 3).reshape(ND, SRC_TILES * TILE).astype(jnp.bfloat16)
    return jnp.dot(dense, source, preferred_element_type=jnp.float32)


def sage_layer(proj, bias, send_rows, tile_dst, tile_src, tile_count, tile_vals):
    self_part = proj[:, :HID]
    neigh = proj[:, HID:].astype(jnp.bfloat16)

    def one_part(part_id):
        senders = jnp.arange(DEVICES, dtype=jnp.int32)[:, None] * ND
        picks = (senders + send_rows[:, part_id, :]).reshape(-1)
        halo = neigh[picks]
        local = lax.dynamic_slice_in_dim(neigh, part_id * ND, ND, 0)
        source = jnp.concatenate([local, halo], axis=0)
        summed = aggregate(tile_vals[part_id], tile_dst[part_id], tile_src[part_id], tile_count[part_id], source)
        return lax.dynamic_slice_in_dim(self_part, part_id * ND, ND, 0) + summed + bias

    return lax.map(one_part, jnp.arange(DEVICES, dtype=jnp.int32)).reshape(-1, HID)


def reference(features, weights1, bias1, weights2, bias2, send_rows, tile_dst, tile_src, tile_count, tile_vals):
    proj1 = jnp.dot(features, weights1, preferred_element_type=jnp.float32)
    hidden1 = jax.nn.relu(sage_layer(proj1, bias1, send_rows, tile_dst, tile_src, tile_count, tile_vals)).astype(jnp.bfloat16)
    proj2 = jnp.dot(hidden1, weights2, preferred_element_type=jnp.float32)
    return sage_layer(proj2, bias2, send_rows, tile_dst, tile_src, tile_count, tile_vals).astype(jnp.bfloat16)
```

```python
import jax
import jax.numpy as jnp
from jax import lax
from jax.sharding import PartitionSpec as P

ND = 1024


def dense_adjacency(vals, dst, src, count):
    pos = dst * 16 + src
    slot = jnp.arange(128, dtype=jnp.int32)
    hit = (pos[None, :] == slot[:, None]) & (slot[None, :] < count)
    inv = jnp.sum(jnp.where(hit, slot[None, :], 0), axis=1)
    live = jnp.any(hit, axis=1)
    tiles = jnp.where(live[:, None, None], vals[inv], 0)
    return tiles.reshape(8, 16, 128, 128).transpose(0, 2, 1, 3).reshape(ND, 2048)


def shards(
    features, weights1, bias1, weights2, bias2, send_rows, tile_dst, tile_src, tile_count, tile_vals
):
    dense = dense_adjacency(tile_vals[0], tile_dst[0], tile_src[0], tile_count[0])
    feats = lax.all_to_all(features.reshape(16, ND, 64), "mp", split_axis=0, concat_axis=0, tiled=True)
    feats = feats.transpose(1, 0, 2).reshape(ND, 1024)
    w1 = lax.all_gather(weights1, "mp", axis=0, tiled=True)
    rows = send_rows[0].reshape(-1)

    def layer(proj, bias):
        neigh = proj[:, 512:].astype(jnp.bfloat16)
        outgoing = neigh[rows].reshape(128, 8, 512)
        arrived = lax.all_to_all(outgoing, ("dp", "mp"), split_axis=0, concat_axis=0, tiled=True)
        source = jnp.concatenate([neigh, arrived.reshape(-1, 512)], axis=0)
        return proj[:, :512] + jnp.dot(dense, source, preferred_element_type=jnp.float32) + bias

    proj1 = jnp.dot(feats, w1, preferred_element_type=jnp.float32)
    hidden1 = jax.nn.relu(layer(proj1, bias1)).astype(jnp.bfloat16)
    proj2 = jnp.dot(hidden1, weights2, preferred_element_type=jnp.float32)
    return layer(proj2, bias2).astype(jnp.bfloat16)


def solution(mesh):
    return jax.shard_map(
        shards,
        mesh=mesh,
        in_specs=(
            P("dp", "mp"),
            P("mp", None),
            P(),
            P(),
            P(),
            P(("dp", "mp"), None, None),
            P(("dp", "mp"), None),
            P(("dp", "mp"), None),
            P(("dp", "mp")),
            P(("dp", "mp"), None, None, None),
        ),
        out_specs=P(("dp", "mp"), None),
        check_vma=False,
    )
```

```python
import jax
import jax.numpy as jnp
from jax import lax
from jax.experimental import pallas as pl
from jax.experimental.pallas import tpu as pltpu
from jax.sharding import PartitionSpec as P

MESH = pl.DeviceIdType.MESH
ND, F, HID, TILE = 1024, 1024, 512, 128
STEPS = (2, 1, 3, 0)
BF = jnp.bfloat16
F32 = jnp.float32


def dot(a, b):
    return jnp.dot(a, b, preferred_element_type=F32)


def dot_t(a, b):
    return lax.dot_general(a, b, (((0,), (0,)), ((), ())), preferred_element_type=F32)


def kernel(
    feat, w1, bias1, w2, bias2, rows, slot, vals, out,
    xt, w1f, w2v, tiles, adj, pick, acc, neigh, hidden, result,
    outgoing1, outgoing2, halo1, halo2,
    local_sem, x_send, x_recv, w_send, w_recv, h_send, h_recv, o_sem,
):
    dp, mp = lax.axis_index("dp"), lax.axis_index("mp")
    x, c, y, z = dp // 2, dp % 2, mp // 4, mp % 4

    def remote(src, dst, send, recv, to):
        return pltpu.make_async_remote_copy(
            src_ref=src, dst_ref=dst, send_sem=send, recv_sem=recv, device_id=to, device_id_type=MESH
        )

    cb = pl.multiple_of((c * 4 + x) * 128, 128)
    mine = [
        pltpu.make_async_copy(vals, tiles.at[pl.ds(0, 128)], local_sem.at[0]),
        pltpu.make_async_copy(w2, w2v, local_sem.at[1]),
        pltpu.make_async_copy(
            feat.at[:, pl.ds(pl.multiple_of(mp * ND, ND), ND)], xt.at[mp], local_sem.at[2]
        ),
        pltpu.make_async_copy(w1.at[:, pl.ds(cb, 128)], w1f.at[mp, :, pl.ds(cb, 128)], local_sem.at[3]),
    ]
    for copy in mine:
        copy.start()

    barrier = pltpu.get_barrier_semaphore()

    @pl.loop(1, 128)
    def _(i):
        there = lax.rem(dp + i // 16, 8), lax.rem(mp + i % 16, 16)
        pl.semaphore_signal(barrier, inc=1, device_id=there, device_id_type=MESH)

    pl.semaphore_wait(barrier, 127)

    @pl.loop(1, 16)
    def _(i):
        there = lax.rem(y + i // 4, 4) * 4 + lax.rem(z + i % 4, 4)
        remote(
            w1.at[:, pl.ds(cb, 128)], w1f.at[mp, :, pl.ds(cb, 128)], w_send.at[0], w_recv.at[0], (dp, there)
        ).start()

    for g, dy in enumerate(STEPS):
        @pl.loop(1 if dy == 0 else 0, 4)
        def _(i):
            there = lax.rem(y + dy, 4) * 4 + lax.rem(z + i, 4)
            block = pl.ds(pl.multiple_of(there * ND, ND), ND)
            remote(feat.at[:, block], xt.at[mp], x_send, x_recv.at[g], (dp, there)).start()

    table = rows[...]
    lanes = lax.broadcasted_iota(jnp.int32, (16, ND), 1)
    for r in range(0, 128, 2):
        want = jnp.concatenate([table[:, r : r + 1], table[:, r + 1 : r + 2]], axis=0)
        pick[r * 8 : r * 8 + 16, :] = jnp.where(want == lanes, 1.0, 0.0).astype(BF)

    mine[3].wait()
    remote(
        w1f.at[pl.ds(0, 15), :, pl.ds(0, 128)], w1f.at[pl.ds(0, 15), :, pl.ds(0, 128)],
        w_send.at[0], w_recv.at[0], (dp, mp),
    ).wait_recv()
    for dx in (1, 2, 3):
        part = w1f.at[:, :, pl.ds(cb, 128)]
        remote(part, part, w_send.at[1], w_recv.at[1], (lax.rem(x + dx, 4) * 2 + c, mp)).start()

    tiles[128] = jnp.zeros((TILE, TILE), BF)
    mine[0].wait()

    @pl.loop(0, 8)
    def _(d):
        at = pl.ds(pl.multiple_of(d * TILE, TILE), TILE)
        for s in range(16):
            adj[at, s * TILE : (s + 1) * TILE] = tiles[slot[d * 16 + s]]

    others = w1f.at[:, :, pl.ds(0, 384)]
    remote(others, others, w_send.at[1], w_recv.at[1], (dp, mp)).wait_recv()
    half = w1f.at[:, :, pl.ds(pl.multiple_of(c * 512, 512), 512)]
    remote(half, half, w_send.at[2], w_recv.at[2], (x * 2 + 1 - c, mp)).start()
    remote(half, half, w_send.at[2], w_recv.at[2], (dp, mp)).wait_recv()
    mine[2].wait()
    mine[1].wait()

    for g, dy in enumerate(STEPS):
        count = 3 if dy == 0 else 4
        part = xt.at[pl.ds(0, count)]
        remote(part, part, x_send, x_recv.at[g], (dp, mp)).wait_recv()
        src = pl.ds(lax.rem(y + 4 - dy, 4) * 4, 4)
        last = g == 3

        def project(col, m):
            at = pl.ds(pl.multiple_of(m * 256, 256), 256)
            got = dot_t(
                xt[src, :, at].reshape(256, 256), w1f[src, :, col : col + 512].reshape(256, 512)
            )
            if g > 0:
                got = got + acc[at, col : col + 512]
            return at, got

        @pl.loop(0, 4)
        def _(m):
            at, got = project(512, m)
            if last:
                neigh[at, :] = got.astype(BF)
            else:
                acc[at, 512:] = got

        if not last:
            @pl.loop(0, 4)
            def _(m):
                at, got = project(0, m)
                acc[at, :512] = got

    def send_halo(layer, outgoing, halo):
        for g, dx in enumerate(STEPS):
            there_x = lax.rem(x + dx, 4)
            at = pl.ds(pl.multiple_of(there_x * 256, 256), 256)
            picked = dot(pick[at, :], neigh[...])
            outgoing[pl.ds(there_x * 32, 32)] = picked.reshape(32, 8, HID).astype(BF)

            @pl.loop(1 if dx == 0 else 0, 32)
            def _(i):
                there_dp = there_x * 2 + lax.rem(c + i % 2, 2)
                there_mp = lax.rem(y + i // 8, 4) * 4 + lax.rem(z + (i // 2) % 4, 4)
                remote(
                    outgoing.at[there_dp * 16 + there_mp], halo.at[dp * 16 + mp],
                    h_send.at[layer], h_recv.at[layer, g], (there_dp, there_mp),
                ).start()

        halo[dp * 16 + mp] = outgoing[dp * 16 + mp]

    def own(bias):
        @pl.loop(0, 4)
        def _(m):
            at = pl.ds(pl.multiple_of(m * 256, 256), 256)
            acc[at, :512] = acc[at, :512] + bias[...] + dot(adj[at, :ND], neigh[...])

    def receive_halo(layer, halo, finish):
        for g, dx in enumerate(STEPS):
            part = halo.at[pl.ds(0, 31 if dx == 0 else 32)]
            remote(part, part, h_send.at[layer], h_recv.at[layer, g], (dp, mp)).wait_recv()
            from_x = lax.rem(x + 4 - dx, 4)
            src = halo[pl.ds(from_x * 32, 32)].reshape(256, HID)
            cols = pl.ds(pl.multiple_of(ND + from_x * 256, 256), 256)

            @pl.loop(0, 4)
            def _(m):
                at = pl.ds(pl.multiple_of(m * 256, 256), 256)
                got = acc[at, :512] + dot(adj[at, cols], src)
                if g == 3:
                    finish(m, at, got)
                else:
                    acc[at, :512] = got

    send_halo(0, outgoing1, halo1)

    @pl.loop(0, 4)
    def _(m):
        at, got = project(0, m)
        acc[at, :512] = got

    own(bias1)

    def finish1(m, at, got):
        hidden[at, :] = jnp.maximum(got, 0.0).astype(BF)

    receive_halo(0, halo1, finish1)

    @pl.loop(0, 4)
    def _(m):
        at = pl.ds(pl.multiple_of(m * 256, 256), 256)
        neigh[at, :] = dot(hidden[at, :], w2v[:, 512:]).astype(BF)

    send_halo(1, outgoing2, halo2)

    @pl.loop(0, 4)
    def _(m):
        at = pl.ds(pl.multiple_of(m * 256, 256), 256)
        acc[at, :512] = dot(hidden[at, :], w2v[:, :512])

    own(bias2)

    def finish2(m, at, got):
        result[at, :] = got.astype(BF)
        pltpu.make_async_copy(result.at[at], out.at[at], o_sem.at[m]).start()

    receive_halo(1, halo2, finish2)

    for m in range(4):
        at = pl.ds(m * 256, 256)
        pltpu.make_async_copy(result.at[at], out.at[at], o_sem.at[m]).wait()

    sent = xt.at[pl.ds(0, 15)]
    remote(sent, sent, x_send, x_recv.at[0], (dp, mp)).wait_send()
    sent = w1f.at[pl.ds(0, 15), :, pl.ds(0, 128)]
    remote(sent, sent, w_send.at[0], w_recv.at[0], (dp, mp)).wait_send()
    remote(others, others, w_send.at[1], w_recv.at[1], (dp, mp)).wait_send()
    remote(half, half, w_send.at[2], w_recv.at[2], (dp, mp)).wait_send()
    for layer, outgoing in enumerate((outgoing1, outgoing2)):
        sent = outgoing.at[pl.ds(0, 127)]
        remote(sent, sent, h_send.at[layer], h_recv.at[layer, 0], (dp, mp)).wait_send()


def shards(
    features, weights1, bias1, weights2, bias2, send_rows, tile_dst, tile_src, tile_count, tile_vals
):
    pos = tile_dst[0] * 16 + tile_src[0]
    place = jnp.arange(128, dtype=jnp.int32)
    hit = (pos[None, :] == place[:, None]) & (place[None, :] < tile_count[0])
    slot = jnp.sum(jnp.where(hit, place[None, :] - 128, 0), axis=1) + 128

    hbm = pl.BlockSpec(memory_space=pl.ANY)
    vmem = pl.BlockSpec(memory_space=pltpu.VMEM)
    smem = pl.BlockSpec(memory_space=pltpu.SMEM)
    dma = pltpu.SemaphoreType.DMA
    return pl.pallas_call(
        kernel,
        out_shape=jax.ShapeDtypeStruct((ND, HID), BF),
        in_specs=[hbm, hbm, vmem, hbm, vmem, vmem, smem, hbm],
        out_specs=hbm,
        scratch_shapes=[
            pltpu.VMEM((16, 64, ND), BF),
            pltpu.VMEM((16, 64, 2 * HID), BF),
            pltpu.VMEM((HID, 2 * HID), BF),
            pltpu.VMEM((129, TILE, TILE), BF),
            pltpu.VMEM((ND, 2 * ND), BF),
            pltpu.VMEM((ND, ND), BF),
            pltpu.VMEM((ND, 2 * HID), F32),
            pltpu.VMEM((ND, HID), BF),
            pltpu.VMEM((ND, HID), BF),
            pltpu.VMEM((ND, HID), BF),
            pltpu.VMEM((128, 8, HID), BF),
            pltpu.VMEM((128, 8, HID), BF),
            pltpu.VMEM((128, 8, HID), BF),
            pltpu.VMEM((128, 8, HID), BF),
            dma((4,)), dma, dma((4,)), dma((3,)), dma((3,)), dma((2,)), dma((2, 4)), dma((4,)),
        ],
        compiler_params=pltpu.CompilerParams(
            collective_id=0, has_side_effects=True, vmem_limit_bytes=56 * 2**20
        ),
    )(
        features.T, weights1, bias1.reshape(1, HID), weights2, bias2.reshape(1, HID),
        send_rows[0].T, slot, tile_vals[0],
    )


def solution(mesh):
    return jax.shard_map(
        shards,
        mesh=mesh,
        in_specs=(
            P("dp", "mp"),
            P("mp", None),
            P(),
            P(),
            P(),
            P(("dp", "mp"), None, None),
            P(("dp", "mp"), None),
            P(("dp", "mp"), None),
            P(("dp", "mp")),
            P(("dp", "mp"), None, None, None),
        ),
        out_specs=P(("dp", "mp"), None),
        check_vma=False,
    )
```

```python
import jax
import jax.numpy as jnp
from jax import lax
from jax.experimental import pallas as pl
from jax.experimental.pallas import tpu as pltpu
from jax.sharding import PartitionSpec as P

MESH = pl.DeviceIdType.MESH
ND, F, HID, TILE = 1024, 1024, 512, 128
STEPS = (2, 1, 3, 0)
PLANE = ((2, 2), (2, 1), (1, 2), (2, 3), (3, 2), (0, 2), (2, 0), (1, 1), (3, 3), (1, 3), (3, 1), (0, 1), (1, 0), (0, 3), (3, 0))
BF = jnp.bfloat16
F32 = jnp.float32


def dot(a, b):
    return jnp.dot(a, b, preferred_element_type=F32)


def dot_t(a, b):
    return lax.dot_general(a, b, (((0,), (0,)), ((), ())), preferred_element_type=F32)


def dot_nt(a, b):
    return lax.dot_general(a, b, (((1,), (1,)), ((), ())), preferred_element_type=F32)


def kernel(
    feat, w1, bias1, w2, bias2, rows, dst, src_tile, count, vals, out,
    xs, xt, w1f, w1t, w2v, tiles, adj, pick, acc, acc_t, neigh_t, neigh, hidden, result, slot_v, slot,
    outgoing1, outgoing2, halo1, halo2,
    local_sem, x_send, x_recv, w_send, w_recv, h_send, h_recv, o_sem,
):
    dp, mp = lax.axis_index("dp"), lax.axis_index("mp")
    x, c, y, z = dp // 2, dp % 2, mp // 4, mp % 4
    xs_at = [lax.rem(x + d, 4) for d in range(4)]
    ys_at = [lax.rem(y + d, 4) * 4 for d in range(4)]
    zs_at = [lax.rem(z + d, 4) for d in range(4)]
    cs_at = [c, 1 - c]

    def remote(src, dst, send, recv, to):
        return pltpu.make_async_remote_copy(
            src_ref=src, dst_ref=dst, send_sem=send, recv_sem=recv, device_id=to, device_id_type=MESH
        )

    barrier = pltpu.get_barrier_semaphore()
    plane = [ys_at[a] + zs_at[b] for a, b in PLANE]
    along_x = [(xs_at[d] * 2 + c, mp) for d in (1, 3, 2)]
    sibling = x * 2 + 1 - c, mp
    for there in [(dp, p) for p in plane] + along_x + [sibling]:
        pl.semaphore_signal(barrier, inc=1, device_id=there, device_id_type=MESH)

    cb = pl.multiple_of((c * 4 + x) * 128, 128)
    w1_mine = pltpu.make_async_copy(w1.at[:, pl.ds(cb, 128)], w1f.at[mp, :, pl.ds(cb, 128)], local_sem.at[0])
    w1_mine.start()
    staged = [
        pltpu.make_async_copy(feat.at[:, pl.ds(p * ND, ND)], xs.at[p], local_sem.at[1]) for p in range(16)
    ]
    for copy in staged:
        copy.start()
    tiles_in = pltpu.make_async_copy(vals, tiles.at[pl.ds(0, 128)], local_sem.at[2])
    tiles_in.start()
    w2_in = pltpu.make_async_copy(w2, w2v, local_sem.at[3])
    w2_in.start()

    place = jnp.broadcast_to(dst[...] * 16 + src_tile[...], (128, 128)).T
    t_iota = lax.broadcasted_iota(jnp.int32, (128, 128), 0)
    q_iota = lax.broadcasted_iota(jnp.int32, (128, 128), 1)
    hit = (place == q_iota) & (t_iota < count[0])
    slot_v[...] = jnp.sum(jnp.where(hit, t_iota - 128, 0), axis=0, keepdims=True) + 128
    slot_in = pltpu.make_async_copy(slot_v, slot, local_sem.at[4])
    slot_in.start()
    tiles[128] = jnp.zeros((TILE, TILE), BF)

    table = rows[...]
    lanes = lax.broadcasted_iota(jnp.int32, (16, ND), 1)
    for r in range(0, 128, 2):
        want = jnp.concatenate([table[:, r : r + 1], table[:, r + 1 : r + 2]], axis=0)
        pick[r * 8 : r * 8 + 16, :] = jnp.where(want == lanes, 1.0, 0.0).astype(BF)

    pltpu.make_async_copy(xs, xs, local_sem.at[1]).wait()
    pl.semaphore_wait(barrier, 19)

    for p in plane:
        remote(
            w1.at[:, pl.ds(cb, 128)], w1f.at[mp, :, pl.ds(cb, 128)], w_send.at[0], w_recv.at[0], (dp, p)
        ).start()

    for (a, b), p in zip(PLANE, plane):
        remote(xs.at[p], xt.at[mp], x_send, x_recv.at[STEPS.index(a)], (dp, p)).start()
    xt_mine = pltpu.make_async_copy(xs.at[mp], xt.at[mp], local_sem.at[5])
    xt_mine.start()

    w1_mine.wait()
    got = w1f.at[pl.ds(0, 15), :, pl.ds(0, 128)]
    remote(got, got, w_send.at[0], w_recv.at[0], (dp, mp)).wait_recv()
    for there in along_x:
        part = w1f.at[:, :, pl.ds(cb, 128)]
        remote(part, part, w_send.at[1], w_recv.at[1], there).start()

    tiles_in.wait()
    slot_in.wait()

    @pl.loop(0, 8)
    def _(d):
        at = pl.ds(pl.multiple_of(d * TILE, TILE), TILE)
        for s in range(16):
            adj[at, s * TILE : (s + 1) * TILE] = tiles[slot[0, d * 16 + s]]

    others = w1f.at[:, :, pl.ds(0, 384)]
    remote(others, others, w_send.at[1], w_recv.at[1], (dp, mp)).wait_recv()
    half = w1f.at[:, :, pl.ds(pl.multiple_of(c * 512, 512), 512)]
    remote(half, half, w_send.at[2], w_recv.at[2], sibling).start()
    remote(half, half, w_send.at[2], w_recv.at[2], (dp, mp)).wait_recv()
    for k in range(4):
        w1t[:, k * 256 : (k + 1) * 256] = w1f[k * 4 : k * 4 + 4, :, 512:].reshape(256, HID).T
    w2_in.wait()
    xt_mine.wait()

    for g, dy in enumerate(STEPS):
        part = xt.at[pl.ds(0, 3 if dy == 0 else 4)]
        remote(part, part, x_send, x_recv.at[g], (dp, mp)).wait_recv()
        from_y = lax.rem(y + 4 - dy, 4)
        weights = w1t[:, pl.ds(pl.multiple_of(from_y * 256, 256), 256)]
        for n in range(0, ND, 512):
            add = dot(weights, xt[pl.ds(from_y * 4, 4), :, n : n + 512].reshape(256, 512))
            if g > 0:
                add = add + acc_t[:, n : n + 512]
            if g < 3:
                acc_t[:, n : n + 512] = add
            else:
                neigh_t[:, n : n + 512] = add.astype(BF)

    def send_halo(layer, picked, outgoing, halo):
        for g, dx in enumerate(STEPS):
            there_x = xs_at[dx]
            at = pl.ds(pl.multiple_of(there_x * 256, 256), 256)
            outgoing[pl.ds(there_x * 32, 32)] = picked(pick[at, :]).reshape(32, 8, HID).astype(BF)
            for a in STEPS:
                for b in STEPS:
                    for e in (1, 0):
                        if (dx, a, b, e) != (0, 0, 0, 0):
                            there_dp, there_mp = there_x * 2 + cs_at[e], ys_at[a] + zs_at[b]
                            remote(
                                outgoing.at[there_dp * 16 + there_mp], halo.at[dp * 16 + mp],
                                h_send.at[layer], h_recv.at[layer, g], (there_dp, there_mp),
                            ).start()
        halo[dp * 16 + mp] = outgoing[dp * 16 + mp]

    def receive_halo(layer, halo, project, finish):
        for g, dx in enumerate(STEPS):
            part = halo.at[pl.ds(0, 31 if dx == 0 else 32)]
            remote(part, part, h_send.at[layer], h_recv.at[layer, g], (dp, mp)).wait_recv()
            from_x = lax.rem(x + 4 - dx, 4)
            src = project(halo[pl.ds(from_x * 32, 32)].reshape(256, HID))
            cols = pl.ds(pl.multiple_of(ND + from_x * 256, 256), 256)
            for m in range(2):
                at = pl.ds(m * 512, 512)
                add = acc[at, :] + dot(adj[at, cols], src)
                if g == 3:
                    finish(m, at, add)
                else:
                    acc[at, :] = add

    send_halo(0, lambda one_hot: dot_nt(one_hot, neigh_t[...]), outgoing1, halo1)

    @pl.loop(0, 4)
    def _(m):
        at = pl.ds(pl.multiple_of(m * 256, 256), 256)
        self_part = dot_t(xt[:, :, at].reshape(ND, 256), w1f[:, :, :512].reshape(F, HID))
        acc[at, :] = self_part + bias1[...] + dot_nt(adj[at, :ND], neigh_t[...])

    def finish1(m, at, add):
        hidden[at, :] = jnp.maximum(add, 0.0).astype(BF)

    receive_halo(0, halo1, lambda block: block, finish1)

    send_halo(1, lambda one_hot: dot(one_hot, hidden[...]), outgoing2, halo2)

    @pl.loop(0, 4)
    def _(m):
        at = pl.ds(pl.multiple_of(m * 256, 256), 256)
        neigh[at, :] = dot(hidden[at, :], w2v[:, 512:]).astype(BF)

    @pl.loop(0, 4)
    def _(m):
        at = pl.ds(pl.multiple_of(m * 256, 256), 256)
        acc[at, :] = dot(hidden[at, :], w2v[:, :512]) + bias2[...] + dot(adj[at, :ND], neigh[...])

    def finish2(m, at, add):
        result[at, :] = add.astype(BF)
        pltpu.make_async_copy(result.at[at], out.at[at], o_sem.at[m]).start()

    receive_halo(1, halo2, lambda block: dot(block, w2v[:, 512:]).astype(BF), finish2)
    for m in range(2):
        at = pl.ds(m * 512, 512)
        pltpu.make_async_copy(result.at[at], out.at[at], o_sem.at[m]).wait()

    sent = xt.at[pl.ds(0, 15)]
    remote(sent, sent, x_send, x_recv.at[0], (dp, mp)).wait_send()
    remote(got, got, w_send.at[0], w_recv.at[0], (dp, mp)).wait_send()
    remote(others, others, w_send.at[1], w_recv.at[1], (dp, mp)).wait_send()
    remote(half, half, w_send.at[2], w_recv.at[2], (dp, mp)).wait_send()
    for layer, outgoing in enumerate((outgoing1, outgoing2)):
        sent = outgoing.at[pl.ds(0, 127)]
        remote(sent, sent, h_send.at[layer], h_recv.at[layer, 0], (dp, mp)).wait_send()


def shards(
    features, weights1, bias1, weights2, bias2, send_rows, tile_dst, tile_src, tile_count, tile_vals
):
    hbm = pl.BlockSpec(memory_space=pl.ANY)
    vmem = pl.BlockSpec(memory_space=pltpu.VMEM)
    smem = pl.BlockSpec(memory_space=pltpu.SMEM)
    dma = pltpu.SemaphoreType.DMA
    return pl.pallas_call(
        kernel,
        out_shape=jax.ShapeDtypeStruct((ND, HID), BF),
        in_specs=[hbm, hbm, vmem, hbm, vmem, vmem, vmem, vmem, smem, hbm],
        out_specs=hbm,
        scratch_shapes=[
            pltpu.VMEM((16, 64, ND), BF),
            pltpu.VMEM((16, 64, ND), BF),
            pltpu.VMEM((16, 64, 2 * HID), BF),
            pltpu.VMEM((HID, F), BF),
            pltpu.VMEM((HID, 2 * HID), BF),
            pltpu.VMEM((129, TILE, TILE), BF),
            pltpu.VMEM((ND, 2 * ND), BF),
            pltpu.VMEM((ND, ND), BF),
            pltpu.VMEM((ND, HID), F32),
            pltpu.VMEM((HID, ND), F32),
            pltpu.VMEM((HID, ND), BF),
            pltpu.VMEM((ND, HID), BF),
            pltpu.VMEM((ND, HID), BF),
            pltpu.VMEM((ND, HID), BF),
            pltpu.VMEM((1, 128), jnp.int32),
            pltpu.SMEM((1, 128), jnp.int32),
            pltpu.VMEM((128, 8, HID), BF),
            pltpu.VMEM((128, 8, HID), BF),
            pltpu.VMEM((128, 8, HID), BF),
            pltpu.VMEM((128, 8, HID), BF),
            dma((6,)), dma, dma((4,)), dma((3,)), dma((3,)), dma((2,)), dma((2, 4)), dma((2,)),
        ],
        compiler_params=pltpu.CompilerParams(
            collective_id=0, has_side_effects=True, vmem_limit_bytes=56 * 2**20
        ),
    )(
        features.T, weights1, bias1.reshape(1, HID), weights2, bias2.reshape(1, HID),
        send_rows[0].T, tile_dst, tile_src, tile_count, tile_vals[0],
    )


def solution(mesh):
    return jax.shard_map(
        shards,
        mesh=mesh,
        in_specs=(
            P("dp", "mp"),
            P("mp", None),
            P(),
            P(),
            P(),
            P(("dp", "mp"), None, None),
            P(("dp", "mp"), None),
            P(("dp", "mp"), None),
            P(("dp", "mp")),
            P(("dp", "mp"), None, None, None),
        ),
        out_specs=P(("dp", "mp"), None),
        check_vma=False,
    )
```

```python
import jax
import jax.numpy as jnp
from jax import lax
from jax.experimental import pallas as pl
from jax.experimental.pallas import tpu as pltpu
from jax.sharding import PartitionSpec as P

MESH = pl.DeviceIdType.MESH
ND, F, HID, TILE = 1024, 1024, 512, 128
STEPS = (2, 1, 3, 0)
PLANE = ((2, 2), (2, 1), (1, 2), (2, 3), (3, 2), (0, 2), (2, 0), (1, 1), (3, 3), (1, 3), (3, 1), (0, 1), (1, 0), (0, 3), (3, 0))
BF = jnp.bfloat16
F32 = jnp.float32


def dot(a, b):
    return jnp.dot(a, b, preferred_element_type=F32)


def dot_t(a, b):
    return lax.dot_general(a, b, (((0,), (0,)), ((), ())), preferred_element_type=F32)


def dot_nt(a, b):
    return lax.dot_general(a, b, (((1,), (1,)), ((), ())), preferred_element_type=F32)


def kernel(
    feat, w1, bias1, w2, bias2, rows, dst, src_tile, count, vals, out,
    xs, xt, w1f, w1t, w1s, w2v, tiles, adj, pick, acc, acc_t, neigh_t, neigh, hidden, result, slot_v, slot,
    outgoing1, outgoing2, halo1, halo2,
    local_sem, x_send, x_recv, w_send, w_recv, h_send, h_recv, o_sem,
):
    dp, mp = lax.axis_index("dp"), lax.axis_index("mp")
    x, c, y, z = dp // 2, dp % 2, mp // 4, mp % 4
    xs_at = [lax.rem(x + d, 4) for d in range(4)]
    ys_at = [lax.rem(y + d, 4) * 4 for d in range(4)]
    zs_at = [lax.rem(z + d, 4) for d in range(4)]
    cs_at = [c, 1 - c]

    def remote(src, dst, send, recv, to):
        return pltpu.make_async_remote_copy(
            src_ref=src, dst_ref=dst, send_sem=send, recv_sem=recv, device_id=to, device_id_type=MESH
        )

    barrier = pltpu.get_barrier_semaphore()
    plane = [ys_at[a] + zs_at[b] for a, b in PLANE]
    along_x = [(xs_at[d] * 2 + c, mp) for d in (1, 3, 2)]
    sibling = x * 2 + 1 - c, mp
    for there in [(dp, p) for p in plane] + along_x + [sibling]:
        pl.semaphore_signal(barrier, inc=1, device_id=there, device_id_type=MESH)

    w_rows = pl.ds(pl.multiple_of(c * 32, 32), 32)
    w1_mine = [
        pltpu.make_async_copy(
            w1.at[w_rows, pl.ds(pl.multiple_of(h * HID + x * 128, 128), 128)],
            w1f.at[h, c, x, mp], local_sem.at[0, h],
        )
        for h in range(2)
    ]
    for copy in w1_mine:
        copy.start()
    staged = [
        pltpu.make_async_copy(feat.at[:, pl.ds(p * ND, ND)], xs.at[p], local_sem.at[1, 0]) for p in range(16)
    ]
    for copy in staged:
        copy.start()
    tiles_in = pltpu.make_async_copy(vals, tiles.at[pl.ds(0, 128)], local_sem.at[2, 0])
    tiles_in.start()
    w2_in = pltpu.make_async_copy(w2, w2v, local_sem.at[3, 0])
    w2_in.start()

    place = jnp.broadcast_to(dst[...] * 16 + src_tile[...], (128, 128)).T
    t_iota = lax.broadcasted_iota(jnp.int32, (128, 128), 0)
    q_iota = lax.broadcasted_iota(jnp.int32, (128, 128), 1)
    hit = (place == q_iota) & (t_iota < count[0])
    slot_v[...] = jnp.sum(jnp.where(hit, t_iota - 128, 0), axis=0, keepdims=True) + 128
    slot_in = pltpu.make_async_copy(slot_v, slot, local_sem.at[4, 0])
    slot_in.start()
    tiles[128] = jnp.zeros((TILE, TILE), BF)

    table = rows[...]
    lanes = lax.broadcasted_iota(jnp.int32, (16, ND), 1)
    for r in range(0, 128, 2):
        want = jnp.concatenate([table[:, r : r + 1], table[:, r + 1 : r + 2]], axis=0)
        pick[r * 8 : r * 8 + 16, :] = jnp.where(want == lanes, 1.0, 0.0).astype(BF)

    pltpu.make_async_copy(xs, xs, local_sem.at[1, 0]).wait()
    pl.semaphore_wait(barrier, 19)

    for h in (1, 0):
        w1_mine[h].wait()
        for p in plane:
            block = w1f.at[h, c, x, mp]
            remote(block, block, w_send.at[0, h], w_recv.at[0, h], (dp, p)).start()

    for (a, b), p in zip(PLANE, plane):
        remote(xs.at[p], xt.at[mp], x_send, x_recv.at[STEPS.index(a)], (dp, p)).start()
    xt_mine = pltpu.make_async_copy(xs.at[mp], xt.at[mp], local_sem.at[5, 0])
    xt_mine.start()

    def w1_phase(phase, h):
        part = (w1f.at[h, c, x, pl.ds(0, 15)], w1f.at[h, c, pl.ds(0, 3)], w1f.at[h, c])[phase]
        return remote(part, part, w_send.at[phase, h], w_recv.at[phase, h], (dp, mp))

    for h in (1, 0):
        w1_phase(0, h).wait_recv()
        for there in along_x:
            part = w1f.at[h, c, x]
            remote(part, part, w_send.at[1, h], w_recv.at[1, h], there).start()

    tiles_in.wait()
    slot_in.wait()

    @pl.loop(0, 8)
    def _(d):
        at = pl.ds(pl.multiple_of(d * TILE, TILE), TILE)
        for s in range(16):
            adj[at, s * TILE : (s + 1) * TILE] = tiles[slot[0, d * 16 + s]]

    for h in (1, 0):
        w1_phase(1, h).wait_recv()
        remote(w1f.at[h, c], w1f.at[h, c], w_send.at[2, h], w_recv.at[2, h], sibling).start()

    def w1_columns(h, k):
        return w1f[h, :, k].swapaxes(0, 1).reshape(F, 128)

    w1_phase(2, 1).wait_recv()
    for k in range(4):
        w1t[k * 128 : (k + 1) * 128, :] = w1_columns(1, k).T
    w2_in.wait()
    xt_mine.wait()

    for g, dy in enumerate(STEPS):
        part = xt.at[pl.ds(0, 3 if dy == 0 else 4)]
        remote(part, part, x_send, x_recv.at[g], (dp, mp)).wait_recv()
        from_y = lax.rem(y + 4 - dy, 4)
        weights = w1t[:, pl.ds(pl.multiple_of(from_y * 256, 256), 256)]
        for n in range(0, ND, 512):
            add = dot(weights, xt[pl.ds(from_y * 4, 4), :, n : n + 512].reshape(256, 512))
            if g > 0:
                add = add + acc_t[:, n : n + 512]
            if g < 3:
                acc_t[:, n : n + 512] = add
            else:
                neigh_t[:, n : n + 512] = add.astype(BF)

    def send_halo(layer, picked, outgoing, halo):
        for g, dx in enumerate(STEPS):
            there_x = xs_at[dx]
            at = pl.ds(pl.multiple_of(there_x * 256, 256), 256)
            outgoing[pl.ds(there_x * 32, 32)] = picked(pick[at, :]).reshape(32, 8, HID).astype(BF)
            for a in STEPS:
                for b in STEPS:
                    for e in (1, 0):
                        if (dx, a, b, e) != (0, 0, 0, 0):
                            there_dp, there_mp = there_x * 2 + cs_at[e], ys_at[a] + zs_at[b]
                            remote(
                                outgoing.at[there_dp * 16 + there_mp], halo.at[dp * 16 + mp],
                                h_send.at[layer], h_recv.at[layer, g], (there_dp, there_mp),
                            ).start()
        halo[dp * 16 + mp] = outgoing[dp * 16 + mp]

    def receive_halo(layer, halo, project, finish):
        for g, dx in enumerate(STEPS):
            part = halo.at[pl.ds(0, 31 if dx == 0 else 32)]
            remote(part, part, h_send.at[layer], h_recv.at[layer, g], (dp, mp)).wait_recv()
            from_x = lax.rem(x + 4 - dx, 4)
            src = project(halo[pl.ds(from_x * 32, 32)].reshape(256, HID))
            cols = pl.ds(pl.multiple_of(ND + from_x * 256, 256), 256)
            for m in range(2):
                at = pl.ds(m * 512, 512)
                add = acc[at, :] + dot(adj[at, cols], src)
                if g == 3:
                    finish(m, at, add)
                else:
                    acc[at, :] = add

    send_halo(0, lambda one_hot: dot_nt(one_hot, neigh_t[...]), outgoing1, halo1)

    w1_phase(2, 0).wait_recv()
    for k in range(4):
        w1s[:, k * 128 : (k + 1) * 128] = w1_columns(0, k)

    @pl.loop(0, 4)
    def _(m):
        at = pl.ds(pl.multiple_of(m * 256, 256), 256)
        self_part = dot_t(xt[:, :, at].reshape(ND, 256), w1s[...])
        acc[at, :] = self_part + bias1[...] + dot_nt(adj[at, :ND], neigh_t[...])

    def finish1(m, at, add):
        hidden[at, :] = jnp.maximum(add, 0.0).astype(BF)

    receive_halo(0, halo1, lambda block: block, finish1)

    send_halo(1, lambda one_hot: dot(one_hot, hidden[...]), outgoing2, halo2)

    @pl.loop(0, 4)
    def _(m):
        at = pl.ds(pl.multiple_of(m * 256, 256), 256)
        neigh[at, :] = dot(hidden[at, :], w2v[:, 512:]).astype(BF)

    @pl.loop(0, 4)
    def _(m):
        at = pl.ds(pl.multiple_of(m * 256, 256), 256)
        acc[at, :] = dot(hidden[at, :], w2v[:, :512]) + bias2[...] + dot(adj[at, :ND], neigh[...])

    def finish2(m, at, add):
        result[at, :] = add.astype(BF)
        pltpu.make_async_copy(result.at[at], out.at[at], o_sem.at[m]).start()

    receive_halo(1, halo2, lambda block: dot(block, w2v[:, 512:]).astype(BF), finish2)
    for m in range(2):
        at = pl.ds(m * 512, 512)
        pltpu.make_async_copy(result.at[at], out.at[at], o_sem.at[m]).wait()

    sent = xt.at[pl.ds(0, 15)]
    remote(sent, sent, x_send, x_recv.at[0], (dp, mp)).wait_send()
    for phase in range(3):
        for h in range(2):
            w1_phase(phase, h).wait_send()
    for layer, outgoing in enumerate((outgoing1, outgoing2)):
        sent = outgoing.at[pl.ds(0, 127)]
        remote(sent, sent, h_send.at[layer], h_recv.at[layer, 0], (dp, mp)).wait_send()


def shards(
    features, weights1, bias1, weights2, bias2, send_rows, tile_dst, tile_src, tile_count, tile_vals
):
    hbm = pl.BlockSpec(memory_space=pl.ANY)
    vmem = pl.BlockSpec(memory_space=pltpu.VMEM)
    smem = pl.BlockSpec(memory_space=pltpu.SMEM)
    dma = pltpu.SemaphoreType.DMA
    return pl.pallas_call(
        kernel,
        out_shape=jax.ShapeDtypeStruct((ND, HID), BF),
        in_specs=[hbm, hbm, vmem, hbm, vmem, vmem, vmem, vmem, smem, hbm],
        out_specs=hbm,
        scratch_shapes=[
            pltpu.VMEM((16, 64, ND), BF),
            pltpu.VMEM((16, 64, ND), BF),
            pltpu.VMEM((2, 2, 4, 16, 32, 128), BF),
            pltpu.VMEM((HID, F), BF),
            pltpu.VMEM((F, HID), BF),
            pltpu.VMEM((HID, 2 * HID), BF),
            pltpu.VMEM((129, TILE, TILE), BF),
            pltpu.VMEM((ND, 2 * ND), BF),
            pltpu.VMEM((ND, ND), BF),
            pltpu.VMEM((ND, HID), F32),
            pltpu.VMEM((HID, ND), F32),
            pltpu.VMEM((HID, ND), BF),
            pltpu.VMEM((ND, HID), BF),
            pltpu.VMEM((ND, HID), BF),
            pltpu.VMEM((ND, HID), BF),
            pltpu.VMEM((1, 128), jnp.int32),
            pltpu.SMEM((1, 128), jnp.int32),
            pltpu.VMEM((128, 8, HID), BF),
            pltpu.VMEM((128, 8, HID), BF),
            pltpu.VMEM((128, 8, HID), BF),
            pltpu.VMEM((128, 8, HID), BF),
            dma((6, 2)), dma, dma((4,)), dma((3, 2)), dma((3, 2)), dma((2,)), dma((2, 4)), dma((2,)),
        ],
        compiler_params=pltpu.CompilerParams(
            collective_id=0, has_side_effects=True, vmem_limit_bytes=56 * 2**20
        ),
    )(
        features.T, weights1, bias1.reshape(1, HID), weights2, bias2.reshape(1, HID),
        send_rows[0].T, tile_dst, tile_src, tile_count, tile_vals[0],
    )


def solution(mesh):
    return jax.shard_map(
        shards,
        mesh=mesh,
        in_specs=(
            P("dp", "mp"),
            P("mp", None),
            P(),
            P(),
            P(),
            P(("dp", "mp"), None, None),
            P(("dp", "mp"), None),
            P(("dp", "mp"), None),
            P(("dp", "mp")),
            P(("dp", "mp"), None, None, None),
        ),
        out_specs=P(("dp", "mp"), None),
        check_vma=False,
    )
```

```python
import jax
import jax.numpy as jnp
from jax import lax
from jax.experimental import pallas as pl
from jax.experimental.pallas import tpu as pltpu
from jax.sharding import PartitionSpec as P

MESH = pl.DeviceIdType.MESH
ND, F, HID, TILE = 1024, 1024, 512, 128
STEPS = (2, 1, 3, 0)
PLANE = ((2, 2), (2, 1), (1, 2), (2, 3), (3, 2), (0, 2), (2, 0), (1, 1), (3, 3), (1, 3), (3, 1), (0, 1), (1, 0), (0, 3), (3, 0))
BF = jnp.bfloat16
F32 = jnp.float32


def dot(a, b):
    return jnp.dot(a, b, preferred_element_type=F32)


def dot_t(a, b):
    return lax.dot_general(a, b, (((0,), (0,)), ((), ())), preferred_element_type=F32)


def dot_nt(a, b):
    return lax.dot_general(a, b, (((1,), (1,)), ((), ())), preferred_element_type=F32)


def kernel(
    feat, w1, bias1, w2, bias2, rows, dst, src_tile, count, vals, out,
    xs, xt, w1f, w1t, w1s, w2v, tiles, adj, pick, acc, acc_t, neigh_t, neigh, hidden, part2, slot_v, slot,
    stage, halo,
    local_sem, x_send, x_recv, w_send, w_recv, h_send, h_recv,
):
    dp, mp = lax.axis_index("dp"), lax.axis_index("mp")
    x, c, y, z = dp // 2, dp % 2, mp // 4, mp % 4
    xs_at = [lax.rem(x + d, 4) for d in range(4)]
    ys_at = [lax.rem(y + d, 4) * 4 for d in range(4)]
    zs_at = [lax.rem(z + d, 4) for d in range(4)]
    cs_at = [c, 1 - c]

    def remote(src, dst, send, recv, to):
        return pltpu.make_async_remote_copy(
            src_ref=src, dst_ref=dst, send_sem=send, recv_sem=recv, device_id=to, device_id_type=MESH
        )

    barrier = pltpu.get_barrier_semaphore()
    plane = [ys_at[a] + zs_at[b] for a, b in PLANE]
    along_x = [(xs_at[d] * 2 + c, mp) for d in (1, 3, 2)]
    sibling = x * 2 + 1 - c, mp
    for there in [(dp, p) for p in plane] + along_x + [sibling]:
        pl.semaphore_signal(barrier, inc=1, device_id=there, device_id_type=MESH)

    w_rows = pl.ds(pl.multiple_of(c * 32, 32), 32)
    w1_mine = [
        pltpu.make_async_copy(
            w1.at[w_rows, pl.ds(pl.multiple_of(h * HID + x * 128, 128), 128)],
            w1f.at[h, c, x, mp], local_sem.at[0, h],
        )
        for h in range(2)
    ]
    for copy in w1_mine:
        copy.start()
    staged = [
        pltpu.make_async_copy(feat.at[:, pl.ds(p * ND, ND)], xs.at[p], local_sem.at[1, 0]) for p in range(16)
    ]
    for copy in staged:
        copy.start()
    tiles_in = pltpu.make_async_copy(vals, tiles.at[pl.ds(0, 128)], local_sem.at[2, 0])
    tiles_in.start()
    w2_in = pltpu.make_async_copy(w2, w2v, local_sem.at[3, 0])
    w2_in.start()

    place = jnp.broadcast_to(dst[...] * 16 + src_tile[...], (128, 128)).T
    t_iota = lax.broadcasted_iota(jnp.int32, (128, 128), 0)
    q_iota = lax.broadcasted_iota(jnp.int32, (128, 128), 1)
    hit = (place == q_iota) & (t_iota < count[0])
    slot_v[...] = jnp.sum(jnp.where(hit, t_iota - 128, 0), axis=0, keepdims=True) + 128
    slot_in = pltpu.make_async_copy(slot_v, slot, local_sem.at[4, 0])
    slot_in.start()
    tiles[128] = jnp.zeros((TILE, TILE), BF)

    table = rows[...]
    lanes = lax.broadcasted_iota(jnp.int32, (16, ND), 1)
    for r in range(0, 128, 2):
        want = jnp.concatenate([table[:, r : r + 1], table[:, r + 1 : r + 2]], axis=0)
        pick[r * 8 : r * 8 + 16, :] = jnp.where(want == lanes, 1.0, 0.0).astype(BF)

    pltpu.make_async_copy(xs, xs, local_sem.at[1, 0]).wait()
    pl.semaphore_wait(barrier, 19)

    for h in (1, 0):
        w1_mine[h].wait()
        for p in plane:
            block = w1f.at[h, c, x, mp]
            remote(block, block, w_send.at[0, h], w_recv.at[0, h], (dp, p)).start()

    for (a, b), p in zip(PLANE, plane):
        remote(xs.at[p], xt.at[mp], x_send, x_recv.at[STEPS.index(a)], (dp, p)).start()
    xt_mine = pltpu.make_async_copy(xs.at[mp], xt.at[mp], local_sem.at[5, 0])
    xt_mine.start()

    def w1_phase(phase, h):
        part = (w1f.at[h, c, x, pl.ds(0, 15)], w1f.at[h, c, pl.ds(0, 3)], w1f.at[h, c])[phase]
        return remote(part, part, w_send.at[phase, h], w_recv.at[phase, h], (dp, mp))

    for h in (1, 0):
        w1_phase(0, h).wait_recv()
        for there in along_x:
            part = w1f.at[h, c, x]
            remote(part, part, w_send.at[1, h], w_recv.at[1, h], there).start()

    tiles_in.wait()
    slot_in.wait()

    @pl.loop(0, 8)
    def _(d):
        at = pl.ds(pl.multiple_of(d * TILE, TILE), TILE)
        for s in range(16):
            adj[at, s * TILE : (s + 1) * TILE] = tiles[slot[0, d * 16 + s]]

    for h in (1, 0):
        w1_phase(1, h).wait_recv()
        remote(w1f.at[h, c], w1f.at[h, c], w_send.at[2, h], w_recv.at[2, h], sibling).start()

    def w1_columns(h, k):
        return w1f[h, :, k].swapaxes(0, 1).reshape(F, 128)

    w1_phase(2, 1).wait_recv()
    for k in range(4):
        w1t[k * 128 : (k + 1) * 128, :] = w1_columns(1, k).T
    w2_in.wait()
    xt_mine.wait()

    for g, dy in enumerate(STEPS):
        part = xt.at[pl.ds(0, 3 if dy == 0 else 4)]
        remote(part, part, x_send, x_recv.at[g], (dp, mp)).wait_recv()
        from_y = lax.rem(y + 4 - dy, 4)
        weights = w1t[:, pl.ds(pl.multiple_of(from_y * 256, 256), 256)]
        if g < 3:
            for n in range(0, ND, 512):
                add = dot(weights, xt[pl.ds(from_y * 4, 4), :, n : n + 512].reshape(256, 512))
                acc_t[:, n : n + 512] = add if g == 0 else add + acc_t[:, n : n + 512]

    def neighbours(h):
        at = pl.ds(h * 256, 256)
        neigh_t[at, :] = (
            acc_t[at, :] + dot(w1t[at, pl.ds(pl.multiple_of(y * 256, 256), 256)], xt[pl.ds(y * 4, 4)].reshape(256, ND))
        ).astype(BF)

    def send_rows(layer, h, picked):
        for g, dx in enumerate(STEPS):
            at = pl.ds(pl.multiple_of(xs_at[dx] * 256, 256), 256)
            stage[layer, h, pl.ds(xs_at[dx] * 32, 32)] = picked(pick[at, :]).reshape(32, 8, 256).astype(BF)
            for a in STEPS:
                for b in STEPS:
                    for e in (1, 0):
                        if (dx, a, b, e) != (0, 0, 0, 0):
                            there_dp, there_mp = xs_at[dx] * 2 + cs_at[e], ys_at[a] + zs_at[b]
                            remote(
                                stage.at[layer, h, there_dp * 16 + there_mp], halo.at[layer, h, dp * 16 + mp],
                                h_send.at[layer, h], h_recv.at[layer, h, g], (there_dp, there_mp),
                            ).start()
        halo[layer, h, dp * 16 + mp] = stage[layer, h, dp * 16 + mp]

    def arrived(layer, h, g):
        part = halo.at[layer, h, pl.ds(0, 31 if g == 3 else 32)]
        remote(part, part, h_send.at[layer, h], h_recv.at[layer, h, g], (dp, mp)).wait_recv()
        from_x = lax.rem(x + 4 - STEPS[g], 4)
        return (
            halo[layer, h, pl.ds(from_x * 32, 32)].reshape(256, 256),
            pl.ds(pl.multiple_of(ND + from_x * 256, 256), 256),
            pl.ds(pl.multiple_of(from_x * 256, 256), 256),
        )

    def own1(h):
        half = pl.ds(h * 256, 256)

        @pl.loop(0, 2)
        def _(m):
            at = pl.ds(pl.multiple_of(m * 512, 512), 512)
            self_part = dot_t(xt[:, :, at].reshape(F, 512), w1s[:, half])
            acc[at, half] = self_part + bias1[:, half] + dot_nt(adj[at, :ND], neigh_t[half, :])

    def picked1(h):
        return lambda one_hot: dot_nt(one_hot, neigh_t[h * 256 : (h + 1) * 256, :])

    neighbours(0)
    send_rows(0, 0, picked1(0))
    neighbours(1)
    send_rows(0, 1, picked1(1))
    w1_phase(2, 0).wait_recv()
    for k in range(4):
        w1s[:, k * 128 : (k + 1) * 128] = w1_columns(0, k)
    own1(0)
    own1(1)

    for h in range(2):
        half = pl.ds(h * 256, 256)
        for g in range(4):
            block, cols, _ = arrived(0, h, g)
            add = acc[:, half] + dot(adj[:, cols], block)
            if g < 3:
                acc[:, half] = add
            else:
                hidden[:, half] = jnp.maximum(add, 0.0).astype(BF)
        send_rows(1, h, lambda one_hot: dot(one_hot, hidden[:, half]))

    @pl.loop(0, 4)
    def _(m):
        at = pl.ds(pl.multiple_of(m * 256, 256), 256)
        neigh[at, :] = dot(hidden[at, :], w2v[:, 512:]).astype(BF)

    @pl.loop(0, 2)
    def _(m):
        at = pl.ds(pl.multiple_of(m * 512, 512), 512)
        acc[at, :] = dot(hidden[at, :], w2v[:, :512]) + bias2[...] + dot(adj[at, :ND], neigh[...])

    for g in range(4):
        block, _, at = arrived(1, 0, g)
        part2[at, :] = dot(block, w2v[:256, 512:])
    for g in range(4):
        block, cols, at = arrived(1, 1, g)
        source = (part2[at, :] + dot(block, w2v[256:, 512:])).astype(BF)
        for m in range(2):
            at = pl.ds(m * 512, 512)
            add = acc[at, :] + dot(adj[at, cols], source)
            if g < 3:
                acc[at, :] = add
            else:
                out[at, :] = add.astype(BF)

    sent = xt.at[pl.ds(0, 15)]
    remote(sent, sent, x_send, x_recv.at[0], (dp, mp)).wait_send()
    for phase in range(3):
        for h in range(2):
            w1_phase(phase, h).wait_send()
    for layer in range(2):
        for h in range(2):
            sent = stage.at[layer, h, pl.ds(0, 127)]
            remote(sent, sent, h_send.at[layer, h], h_recv.at[layer, h, 0], (dp, mp)).wait_send()


def shards(
    features, weights1, bias1, weights2, bias2, send_rows, tile_dst, tile_src, tile_count, tile_vals
):
    hbm = pl.BlockSpec(memory_space=pl.ANY)
    vmem = pl.BlockSpec(memory_space=pltpu.VMEM)
    smem = pl.BlockSpec(memory_space=pltpu.SMEM)
    dma = pltpu.SemaphoreType.DMA
    keep = lambda a: pltpu.with_memory_space_constraint(a, pltpu.HBM)
    return pl.pallas_call(
        kernel,
        out_shape=jax.ShapeDtypeStruct((ND, HID), BF),
        in_specs=[hbm, hbm, vmem, hbm, vmem, vmem, vmem, vmem, smem, hbm],
        out_specs=vmem,
        scratch_shapes=[
            pltpu.VMEM((16, 64, ND), BF),
            pltpu.VMEM((16, 64, ND), BF),
            pltpu.VMEM((2, 2, 4, 16, 32, 128), BF),
            pltpu.VMEM((HID, F), BF),
            pltpu.VMEM((F, HID), BF),
            pltpu.VMEM((HID, 2 * HID), BF),
            pltpu.VMEM((129, TILE, TILE), BF),
            pltpu.VMEM((ND, 2 * ND), BF),
            pltpu.VMEM((ND, ND), BF),
            pltpu.VMEM((ND, HID), F32),
            pltpu.VMEM((HID, ND), F32),
            pltpu.VMEM((HID, ND), BF),
            pltpu.VMEM((ND, HID), BF),
            pltpu.VMEM((ND, HID), BF),
            pltpu.VMEM((ND, HID), F32),
            pltpu.VMEM((1, 128), jnp.int32),
            pltpu.SMEM((1, 128), jnp.int32),
            pltpu.VMEM((2, 2, 128, 8, 256), BF),
            pltpu.VMEM((2, 2, 128, 8, 256), BF),
            dma((6, 2)), dma, dma((4,)), dma((3, 2)), dma((3, 2)), dma((2, 2)), dma((2, 2, 4)),
        ],
        compiler_params=pltpu.CompilerParams(
            collective_id=0, has_side_effects=True, vmem_limit_bytes=48 * 2**20
        ),
    )(
        keep(features.T), keep(weights1), keep(bias1.reshape(1, HID)), keep(weights2), keep(bias2.reshape(1, HID)),
        keep(send_rows[0].T), keep(tile_dst), keep(tile_src), tile_count, keep(tile_vals[0]),
    )


def solution(mesh):
    return jax.shard_map(
        shards,
        mesh=mesh,
        in_specs=(
            P("dp", "mp"),
            P("mp", None),
            P(),
            P(),
            P(),
            P(("dp", "mp"), None, None),
            P(("dp", "mp"), None),
            P(("dp", "mp"), None),
            P(("dp", "mp")),
            P(("dp", "mp"), None, None, None),
        ),
        out_specs=P(("dp", "mp"), None),
        check_vma=False,
    )
```

```python
import jax
import jax.numpy as jnp
from jax import lax
from jax.experimental import pallas as pl
from jax.experimental.pallas import tpu as pltpu
from jax.sharding import PartitionSpec as P

MESH = pl.DeviceIdType.MESH
ND, F, HID, TILE = 1024, 1024, 512, 128
STEPS = (2, 1, 3, 0)
PLANE = ((2, 2), (2, 1), (1, 2), (2, 3), (3, 2), (0, 2), (2, 0), (1, 1), (3, 3), (1, 3), (3, 1), (0, 1), (1, 0), (0, 3), (3, 0))
E1, E2 = 9, 12
BF = jnp.bfloat16
F32 = jnp.float32


def dot(a, b):
    return jnp.dot(a, b, preferred_element_type=F32)


def dot_t(a, b):
    return lax.dot_general(a, b, (((0,), (0,)), ((), ())), preferred_element_type=F32)


def dot_nt(a, b):
    return lax.dot_general(a, b, (((1,), (1,)), ((), ())), preferred_element_type=F32)


def kernel(
    feat, w1, bias1, w2, bias2, rows, dst, src_tile, count, vals, out,
    xs, xt, w1f, w1t, w1s, w2v, tiles, adj, pick, acc, acc_t, neigh_t, neigh, hidden, part2, slot_v, slot,
    stage, halo,
    local_sem, x_send, x_recv, w_send, w_recv, h_send, h_recv,
):
    dp, mp = lax.axis_index("dp"), lax.axis_index("mp")
    x, c, y, z = dp // 2, dp % 2, mp // 4, mp % 4
    xs_at = [lax.rem(x + d, 4) for d in range(4)]
    ys_at = [lax.rem(y + d, 4) * 4 for d in range(4)]
    zs_at = [lax.rem(z + d, 4) for d in range(4)]
    cs_at = [c, 1 - c]

    def remote(src, dst, send, recv, to):
        return pltpu.make_async_remote_copy(
            src_ref=src, dst_ref=dst, send_sem=send, recv_sem=recv, device_id=to, device_id_type=MESH
        )

    barrier = pltpu.get_barrier_semaphore()
    plane = [ys_at[a] + zs_at[b] for a, b in PLANE]
    along_x = [(xs_at[d] * 2 + c, mp) for d in (1, 3, 2)]
    sibling = x * 2 + 1 - c, mp
    for there in [(dp, p) for p in plane] + along_x + [sibling]:
        pl.semaphore_signal(barrier, inc=1, device_id=there, device_id_type=MESH)

    w_rows = pl.ds(pl.multiple_of(c * 32, 32), 32)
    w1_mine = [
        pltpu.make_async_copy(
            w1.at[w_rows, pl.ds(pl.multiple_of(h * HID + x * 128, 128), 128)],
            w1f.at[h, c, x, mp], local_sem.at[0, h],
        )
        for h in range(2)
    ]
    for copy in w1_mine:
        copy.start()
    staged = [
        pltpu.make_async_copy(feat.at[:, pl.ds(p * ND, ND)], xs.at[p], local_sem.at[1, 0]) for p in range(16)
    ]
    for copy in staged:
        copy.start()
    tiles_in = pltpu.make_async_copy(vals, tiles.at[pl.ds(0, 128)], local_sem.at[2, 0])
    tiles_in.start()
    w2_in = pltpu.make_async_copy(w2, w2v, local_sem.at[3, 0])
    w2_in.start()

    place = jnp.broadcast_to(dst[...] * 16 + src_tile[...], (128, 128)).T
    t_iota = lax.broadcasted_iota(jnp.int32, (128, 128), 0)
    q_iota = lax.broadcasted_iota(jnp.int32, (128, 128), 1)
    hit = (place == q_iota) & (t_iota < count[0])
    slot_v[...] = jnp.sum(jnp.where(hit, t_iota - 128, 0), axis=0, keepdims=True) + 128
    slot_in = pltpu.make_async_copy(slot_v, slot, local_sem.at[4, 0])
    slot_in.start()
    tiles[128] = jnp.zeros((TILE, TILE), BF)

    table = rows[...]
    lanes = lax.broadcasted_iota(jnp.int32, (16, ND), 1)
    for r in range(0, 128, 2):
        want = jnp.concatenate([table[:, r : r + 1], table[:, r + 1 : r + 2]], axis=0)
        pick[r * 8 : r * 8 + 16, :] = jnp.where(want == lanes, 1.0, 0.0).astype(BF)

    pltpu.make_async_copy(xs, xs, local_sem.at[1, 0]).wait()
    pl.semaphore_wait(barrier, 19)

    for h in (1, 0):
        w1_mine[h].wait()
        for p in plane:
            block = w1f.at[h, c, x, mp]
            remote(block, block, w_send.at[0, h], w_recv.at[0, h], (dp, p)).start()

    def send_features(first, end):
        for (a, b), p in list(zip(PLANE, plane))[first:end]:
            remote(xs.at[p], xt.at[mp], x_send, x_recv.at[STEPS.index(a)], (dp, p)).start()

    send_features(0, E1)
    xt_mine = pltpu.make_async_copy(xs.at[mp], xt.at[mp], local_sem.at[5, 0])
    xt_mine.start()

    def w1_phase(phase, h):
        part = (w1f.at[h, c, x, pl.ds(0, 15)], w1f.at[h, c, pl.ds(0, 3)], w1f.at[h, c])[phase]
        return remote(part, part, w_send.at[phase, h], w_recv.at[phase, h], (dp, mp))

    for h in (1, 0):
        w1_phase(0, h).wait_recv()
        for there in along_x:
            part = w1f.at[h, c, x]
            remote(part, part, w_send.at[1, h], w_recv.at[1, h], there).start()
        if h == 1:
            send_features(E1, E2)

    tiles_in.wait()
    slot_in.wait()

    @pl.loop(0, 8)
    def _(d):
        at = pl.ds(pl.multiple_of(d * TILE, TILE), TILE)
        for s in range(16):
            adj[at, s * TILE : (s + 1) * TILE] = tiles[slot[0, d * 16 + s]]

    for h in (1, 0):
        w1_phase(1, h).wait_recv()
        remote(w1f.at[h, c], w1f.at[h, c], w_send.at[2, h], w_recv.at[2, h], sibling).start()
        if h == 1:
            send_features(E2, 15)

    def w1_columns(h, k):
        return w1f[h, :, k].swapaxes(0, 1).reshape(F, 128)

    w1_phase(2, 1).wait_recv()
    for k in range(4):
        w1t[k * 128 : (k + 1) * 128, :] = w1_columns(1, k).T
    w2_in.wait()
    xt_mine.wait()

    for g, dy in enumerate(STEPS):
        part = xt.at[pl.ds(0, 3 if dy == 0 else 4)]
        remote(part, part, x_send, x_recv.at[g], (dp, mp)).wait_recv()
        from_y = lax.rem(y + 4 - dy, 4)
        weights = w1t[:, pl.ds(pl.multiple_of(from_y * 256, 256), 256)]
        if g < 3:
            for n in range(0, ND, 512):
                add = dot(weights, xt[pl.ds(from_y * 4, 4), :, n : n + 512].reshape(256, 512))
                acc_t[:, n : n + 512] = add if g == 0 else add + acc_t[:, n : n + 512]

    def neighbours(h):
        at = pl.ds(h * 256, 256)
        neigh_t[at, :] = (
            acc_t[at, :] + dot(w1t[at, pl.ds(pl.multiple_of(y * 256, 256), 256)], xt[pl.ds(y * 4, 4)].reshape(256, ND))
        ).astype(BF)

    def send_rows(layer, h, picked):
        for g, dx in enumerate(STEPS):
            at = pl.ds(pl.multiple_of(xs_at[dx] * 256, 256), 256)
            stage[layer, h, pl.ds(xs_at[dx] * 32, 32)] = picked(pick[at, :]).reshape(32, 8, 256).astype(BF)
            for a in STEPS:
                for b in STEPS:
                    for e in (1, 0):
                        if (dx, a, b, e) != (0, 0, 0, 0):
                            there_dp, there_mp = xs_at[dx] * 2 + cs_at[e], ys_at[a] + zs_at[b]
                            remote(
                                stage.at[layer, h, there_dp * 16 + there_mp], halo.at[layer, h, dp * 16 + mp],
                                h_send.at[layer, h], h_recv.at[layer, h, g], (there_dp, there_mp),
                            ).start()
        halo[layer, h, dp * 16 + mp] = stage[layer, h, dp * 16 + mp]

    def arrived(layer, h, g):
        part = halo.at[layer, h, pl.ds(0, 31 if g == 3 else 32)]
        remote(part, part, h_send.at[layer, h], h_recv.at[layer, h, g], (dp, mp)).wait_recv()
        from_x = lax.rem(x + 4 - STEPS[g], 4)
        return (
            halo[layer, h, pl.ds(from_x * 32, 32)].reshape(256, 256),
            pl.ds(pl.multiple_of(ND + from_x * 256, 256), 256),
            pl.ds(pl.multiple_of(from_x * 256, 256), 256),
        )

    def own1(h):
        half = pl.ds(h * 256, 256)

        @pl.loop(0, 2)
        def _(m):
            at = pl.ds(pl.multiple_of(m * 512, 512), 512)
            self_part = dot_t(xt[:, :, at].reshape(F, 512), w1s[:, half])
            acc[at, half] = self_part + bias1[:, half] + dot_nt(adj[at, :ND], neigh_t[half, :])

    def picked1(h):
        return lambda one_hot: dot_nt(one_hot, neigh_t[h * 256 : (h + 1) * 256, :])

    neighbours(0)
    send_rows(0, 0, picked1(0))
    neighbours(1)
    send_rows(0, 1, picked1(1))
    w1_phase(2, 0).wait_recv()
    for k in range(4):
        w1s[:, k * 128 : (k + 1) * 128] = w1_columns(0, k)
    own1(0)
    own1(1)

    for h in range(2):
        half = pl.ds(h * 256, 256)
        for g in range(4):
            block, cols, _ = arrived(0, h, g)
            add = acc[:, half] + dot(adj[:, cols], block)
            if g < 3:
                acc[:, half] = add
            else:
                hidden[:, half] = jnp.maximum(add, 0.0).astype(BF)
        send_rows(1, h, lambda one_hot: dot(one_hot, hidden[:, half]))

    @pl.loop(0, 4)
    def _(m):
        at = pl.ds(pl.multiple_of(m * 256, 256), 256)
        neigh[at, :] = dot(hidden[at, :], w2v[:, 512:]).astype(BF)

    @pl.loop(0, 2)
    def _(m):
        at = pl.ds(pl.multiple_of(m * 512, 512), 512)
        acc[at, :] = dot(hidden[at, :], w2v[:, :512]) + bias2[...] + dot(adj[at, :ND], neigh[...])

    for g in range(4):
        block, _, at = arrived(1, 0, g)
        part2[at, :] = dot(block, w2v[:256, 512:])
    for g in range(4):
        block, cols, at = arrived(1, 1, g)
        source = (part2[at, :] + dot(block, w2v[256:, 512:])).astype(BF)
        for m in range(2):
            at = pl.ds(m * 512, 512)
            add = acc[at, :] + dot(adj[at, cols], source)
            if g < 3:
                acc[at, :] = add
            else:
                out[at, :] = add.astype(BF)

    sent = xt.at[pl.ds(0, 15)]
    remote(sent, sent, x_send, x_recv.at[0], (dp, mp)).wait_send()
    for phase in range(3):
        for h in range(2):
            w1_phase(phase, h).wait_send()
    for layer in range(2):
        for h in range(2):
            sent = stage.at[layer, h, pl.ds(0, 127)]
            remote(sent, sent, h_send.at[layer, h], h_recv.at[layer, h, 0], (dp, mp)).wait_send()


def shards(
    features, weights1, bias1, weights2, bias2, send_rows, tile_dst, tile_src, tile_count, tile_vals
):
    hbm = pl.BlockSpec(memory_space=pl.ANY)
    vmem = pl.BlockSpec(memory_space=pltpu.VMEM)
    smem = pl.BlockSpec(memory_space=pltpu.SMEM)
    dma = pltpu.SemaphoreType.DMA
    keep = lambda a: pltpu.with_memory_space_constraint(a, pltpu.HBM)
    return pl.pallas_call(
        kernel,
        out_shape=jax.ShapeDtypeStruct((ND, HID), BF),
        in_specs=[hbm, hbm, vmem, hbm, vmem, vmem, vmem, vmem, smem, hbm],
        out_specs=vmem,
        scratch_shapes=[
            pltpu.VMEM((16, 64, ND), BF),
            pltpu.VMEM((16, 64, ND), BF),
            pltpu.VMEM((2, 2, 4, 16, 32, 128), BF),
            pltpu.VMEM((HID, F), BF),
            pltpu.VMEM((F, HID), BF),
            pltpu.VMEM((HID, 2 * HID), BF),
            pltpu.VMEM((129, TILE, TILE), BF),
            pltpu.VMEM((ND, 2 * ND), BF),
            pltpu.VMEM((ND, ND), BF),
            pltpu.VMEM((ND, HID), F32),
            pltpu.VMEM((HID, ND), F32),
            pltpu.VMEM((HID, ND), BF),
            pltpu.VMEM((ND, HID), BF),
            pltpu.VMEM((ND, HID), BF),
            pltpu.VMEM((ND, HID), F32),
            pltpu.VMEM((1, 128), jnp.int32),
            pltpu.SMEM((1, 128), jnp.int32),
            pltpu.VMEM((2, 2, 128, 8, 256), BF),
            pltpu.VMEM((2, 2, 128, 8, 256), BF),
            dma((6, 2)), dma, dma((4,)), dma((3, 2)), dma((3, 2)), dma((2, 2)), dma((2, 2, 4)),
        ],
        compiler_params=pltpu.CompilerParams(
            collective_id=0, has_side_effects=True, vmem_limit_bytes=48 * 2**20
        ),
    )(
        keep(features.T), keep(weights1), keep(bias1.reshape(1, HID)), keep(weights2), keep(bias2.reshape(1, HID)),
        keep(send_rows[0].T), keep(tile_dst), keep(tile_src), tile_count, keep(tile_vals[0]),
    )


def solution(mesh):
    return jax.shard_map(
        shards,
        mesh=mesh,
        in_specs=(
            P("dp", "mp"),
            P("mp", None),
            P(),
            P(),
            P(),
            P(("dp", "mp"), None, None),
            P(("dp", "mp"), None),
            P(("dp", "mp"), None),
            P(("dp", "mp")),
            P(("dp", "mp"), None, None, None),
        ),
        out_specs=P(("dp", "mp"), None),
        check_vma=False,
    )
```

```python
import jax
import jax.numpy as jnp
from jax import lax
from jax.experimental import pallas as pl
from jax.experimental.pallas import tpu as pltpu
from jax.sharding import PartitionSpec as P

MESH = pl.DeviceIdType.MESH
ND, F, HID, TILE = 1024, 1024, 512, 128
STEPS = (2, 1, 3, 0)
PLANE = ((2, 2), (2, 1), (1, 2), (2, 3), (3, 2), (0, 2), (2, 0), (1, 1), (3, 3), (1, 3), (3, 1), (0, 1), (1, 0), (0, 3), (3, 0))
E1, E2 = 9, 12
BF = jnp.bfloat16
F32 = jnp.float32


def dot(a, b):
    return jnp.dot(a, b, preferred_element_type=F32)


def dot_t(a, b):
    return lax.dot_general(a, b, (((0,), (0,)), ((), ())), preferred_element_type=F32)


def dot_nt(a, b):
    return lax.dot_general(a, b, (((1,), (1,)), ((), ())), preferred_element_type=F32)


def kernel(
    feat, w1, bias1, w2, bias2, rows, dst, src_tile, count, vals, out,
    xs, xt, w1f, w1t, w1s, w2v, tiles, adj, pick, acc, acc_t, neigh_t, neigh, hidden, part2, slot_v, slot,
    stage, halo,
    local_sem, x_send, x_recv, w_send, w_recv, h_send, h_recv,
):
    dp, mp = lax.axis_index("dp"), lax.axis_index("mp")
    x, c, y, z = dp // 2, dp % 2, mp // 4, mp % 4
    xs_at = [lax.rem(x + d, 4) for d in range(4)]
    ys_at = [lax.rem(y + d, 4) * 4 for d in range(4)]
    zs_at = [lax.rem(z + d, 4) for d in range(4)]
    cs_at = [c, 1 - c]

    def remote(src, dst, send, recv, to):
        return pltpu.make_async_remote_copy(
            src_ref=src, dst_ref=dst, send_sem=send, recv_sem=recv, device_id=to, device_id_type=MESH
        )

    barrier = pltpu.get_barrier_semaphore()
    plane = [ys_at[a] + zs_at[b] for a, b in PLANE]
    along_x = [(xs_at[d] * 2 + c, mp) for d in (1, 3, 2)]
    sibling = x * 2 + 1 - c, mp
    for there in [(dp, p) for p in plane] + along_x + [sibling]:
        pl.semaphore_signal(barrier, inc=1, device_id=there, device_id_type=MESH)

    w_rows = pl.ds(pl.multiple_of(c * 32, 32), 32)
    w1_mine = [
        pltpu.make_async_copy(
            w1.at[w_rows, pl.ds(pl.multiple_of(h * HID + x * 128, 128), 128)],
            w1f.at[h, c, x, mp], local_sem.at[0, h],
        )
        for h in range(2)
    ]
    for copy in w1_mine:
        copy.start()
    staged = [
        pltpu.make_async_copy(feat.at[:, pl.ds(p * ND, ND)], xs.at[p], local_sem.at[1, 0]) for p in range(16)
    ]
    for copy in staged:
        copy.start()
    tiles_in = pltpu.make_async_copy(vals, tiles.at[pl.ds(0, 128)], local_sem.at[2, 0])
    tiles_in.start()
    w2_in = pltpu.make_async_copy(w2, w2v, local_sem.at[3, 0])
    w2_in.start()

    place = jnp.broadcast_to(dst[...] * 16 + src_tile[...], (128, 128)).T
    t_iota = lax.broadcasted_iota(jnp.int32, (128, 128), 0)
    q_iota = lax.broadcasted_iota(jnp.int32, (128, 128), 1)
    hit = (place == q_iota) & (t_iota < count[0])
    slot_v[...] = jnp.sum(jnp.where(hit, t_iota - 128, 0), axis=0, keepdims=True) + 128
    slot_in = pltpu.make_async_copy(slot_v, slot, local_sem.at[4, 0])
    slot_in.start()
    tiles[128] = jnp.zeros((TILE, TILE), BF)

    table = rows[...]
    lanes = lax.broadcasted_iota(jnp.int32, (16, ND), 1)
    for r in range(0, 128, 2):
        want = jnp.concatenate([table[:, r : r + 1], table[:, r + 1 : r + 2]], axis=0)
        pick[r * 8 : r * 8 + 16, :] = jnp.where(want == lanes, 1.0, 0.0).astype(BF)

    pltpu.make_async_copy(xs, xs, local_sem.at[1, 0]).wait()
    pl.semaphore_wait(barrier, 19)

    for h in (1, 0):
        w1_mine[h].wait()
        for p in plane:
            block = w1f.at[h, c, x, mp]
            remote(block, block, w_send.at[0, h], w_recv.at[0, h], (dp, p)).start()

    def send_features(first, end):
        for (a, b), p in list(zip(PLANE, plane))[first:end]:
            remote(xs.at[p], xt.at[mp], x_send, x_recv.at[STEPS.index(a)], (dp, p)).start()

    send_features(0, E1)
    xt_mine = pltpu.make_async_copy(xs.at[mp], xt.at[mp], local_sem.at[5, 0])
    xt_mine.start()

    def w1_phase(phase, h):
        part = (w1f.at[h, c, x, pl.ds(0, 15)], w1f.at[h, c, pl.ds(0, 3)], w1f.at[h, c])[phase]
        return remote(part, part, w_send.at[phase, h], w_recv.at[phase, h], (dp, mp))

    for h in (1, 0):
        w1_phase(0, h).wait_recv()
        for there in along_x:
            part = w1f.at[h, c, x]
            remote(part, part, w_send.at[1, h], w_recv.at[1, h], there).start()
        if h == 1:
            send_features(E1, E2)

    tiles_in.wait()
    slot_in.wait()

    @pl.loop(0, 8)
    def _(d):
        at = pl.ds(pl.multiple_of(d * TILE, TILE), TILE)
        for s in range(16):
            adj[at, s * TILE : (s + 1) * TILE] = tiles[slot[0, d * 16 + s]]

    for h in (1, 0):
        w1_phase(1, h).wait_recv()
        remote(w1f.at[h, c], w1f.at[h, c], w_send.at[2, h], w_recv.at[2, h], sibling).start()
        if h == 1:
            send_features(E2, 15)

    def w1_columns(h, k):
        return w1f[h, :, k].swapaxes(0, 1).reshape(F, 128)

    w1_phase(2, 1).wait_recv()
    for k in range(4):
        w1t[k * 128 : (k + 1) * 128, :] = w1_columns(1, k).T
    w2_in.wait()
    xt_mine.wait()

    for g, dy in enumerate(STEPS):
        part = xt.at[pl.ds(0, 3 if dy == 0 else 4)]
        remote(part, part, x_send, x_recv.at[g], (dp, mp)).wait_recv()
        from_y = lax.rem(y + 4 - dy, 4)
        weights = w1t[:, pl.ds(pl.multiple_of(from_y * 256, 256), 256)]
        if g < 3:
            for n in range(0, ND, 512):
                add = dot(weights, xt[pl.ds(from_y * 4, 4), :, n : n + 512].reshape(256, 512))
                acc_t[:, n : n + 512] = add if g == 0 else add + acc_t[:, n : n + 512]

    def neighbours(h):
        at = pl.ds(h * 256, 256)
        neigh_t[at, :] = (
            acc_t[at, :] + dot(w1t[at, pl.ds(pl.multiple_of(y * 256, 256), 256)], xt[pl.ds(y * 4, 4)].reshape(256, ND))
        ).astype(BF)

    def send_rows(layer, h, picked):
        for g, dx in enumerate(STEPS):
            at = pl.ds(pl.multiple_of(xs_at[dx] * 256, 256), 256)
            stage[layer, h, pl.ds(xs_at[dx] * 32, 32)] = picked(pick[at, :]).reshape(32, 8, 256).astype(BF)
            for e in (1, 0):
                for a, b in PLANE + ((0, 0),):
                    if (dx, a, b, e) != (0, 0, 0, 0):
                        there_dp, there_mp = xs_at[dx] * 2 + cs_at[e], ys_at[a] + zs_at[b]
                        remote(
                            stage.at[layer, h, there_dp * 16 + there_mp], halo.at[layer, h, dp * 16 + mp],
                            h_send.at[layer, h], h_recv.at[layer, h, g], (there_dp, there_mp),
                        ).start()
        halo[layer, h, dp * 16 + mp] = stage[layer, h, dp * 16 + mp]

    def arrived(layer, h, g):
        part = halo.at[layer, h, pl.ds(0, 31 if g == 3 else 32)]
        remote(part, part, h_send.at[layer, h], h_recv.at[layer, h, g], (dp, mp)).wait_recv()
        from_x = lax.rem(x + 4 - STEPS[g], 4)
        return (
            halo[layer, h, pl.ds(from_x * 32, 32)].reshape(256, 256),
            pl.ds(pl.multiple_of(ND + from_x * 256, 256), 256),
            pl.ds(pl.multiple_of(from_x * 256, 256), 256),
        )

    def own1(h):
        half = pl.ds(h * 256, 256)

        @pl.loop(0, 2)
        def _(m):
            at = pl.ds(pl.multiple_of(m * 512, 512), 512)
            self_part = dot_t(xt[:, :, at].reshape(F, 512), w1s[:, half])
            acc[at, half] = self_part + bias1[:, half] + dot_nt(adj[at, :ND], neigh_t[half, :])

    def picked1(h):
        return lambda one_hot: dot_nt(one_hot, neigh_t[h * 256 : (h + 1) * 256, :])

    neighbours(0)
    send_rows(0, 0, picked1(0))
    neighbours(1)
    send_rows(0, 1, picked1(1))
    w1_phase(2, 0).wait_recv()
    for k in range(4):
        w1s[:, k * 128 : (k + 1) * 128] = w1_columns(0, k)
    own1(0)
    own1(1)

    for h in range(2):
        half = pl.ds(h * 256, 256)
        for g in range(4):
            block, cols, _ = arrived(0, h, g)
            add = acc[:, half] + dot(adj[:, cols], block)
            if g < 3:
                acc[:, half] = add
            else:
                hidden[:, half] = jnp.maximum(add, 0.0).astype(BF)
        send_rows(1, h, lambda one_hot: dot(one_hot, hidden[:, half]))

    @pl.loop(0, 4)
    def _(m):
        at = pl.ds(pl.multiple_of(m * 256, 256), 256)
        neigh[at, :] = dot(hidden[at, :], w2v[:, 512:]).astype(BF)

    @pl.loop(0, 2)
    def _(m):
        at = pl.ds(pl.multiple_of(m * 512, 512), 512)
        acc[at, :] = dot(hidden[at, :], w2v[:, :512]) + bias2[...] + dot(adj[at, :ND], neigh[...])

    for g in range(4):
        block, _, at = arrived(1, 0, g)
        part2[at, :] = dot(block, w2v[:256, 512:])
    for g in range(4):
        block, cols, at = arrived(1, 1, g)
        source = (part2[at, :] + dot(block, w2v[256:, 512:])).astype(BF)
        for m in range(2):
            at = pl.ds(m * 512, 512)
            add = acc[at, :] + dot(adj[at, cols], source)
            if g < 3:
                acc[at, :] = add
            else:
                out[at, :] = add.astype(BF)

    sent = xt.at[pl.ds(0, 15)]
    remote(sent, sent, x_send, x_recv.at[0], (dp, mp)).wait_send()
    for phase in range(3):
        for h in range(2):
            w1_phase(phase, h).wait_send()
    for layer in range(2):
        for h in range(2):
            sent = stage.at[layer, h, pl.ds(0, 127)]
            remote(sent, sent, h_send.at[layer, h], h_recv.at[layer, h, 0], (dp, mp)).wait_send()


def shards(
    features, weights1, bias1, weights2, bias2, send_rows, tile_dst, tile_src, tile_count, tile_vals
):
    hbm = pl.BlockSpec(memory_space=pl.ANY)
    vmem = pl.BlockSpec(memory_space=pltpu.VMEM)
    smem = pl.BlockSpec(memory_space=pltpu.SMEM)
    dma = pltpu.SemaphoreType.DMA
    keep = lambda a: pltpu.with_memory_space_constraint(a, pltpu.HBM)
    return pl.pallas_call(
        kernel,
        out_shape=jax.ShapeDtypeStruct((ND, HID), BF),
        in_specs=[hbm, hbm, vmem, hbm, vmem, vmem, vmem, vmem, smem, hbm],
        out_specs=vmem,
        scratch_shapes=[
            pltpu.VMEM((16, 64, ND), BF),
            pltpu.VMEM((16, 64, ND), BF),
            pltpu.VMEM((2, 2, 4, 16, 32, 128), BF),
            pltpu.VMEM((HID, F), BF),
            pltpu.VMEM((F, HID), BF),
            pltpu.VMEM((HID, 2 * HID), BF),
            pltpu.VMEM((129, TILE, TILE), BF),
            pltpu.VMEM((ND, 2 * ND), BF),
            pltpu.VMEM((ND, ND), BF),
            pltpu.VMEM((ND, HID), F32),
            pltpu.VMEM((HID, ND), F32),
            pltpu.VMEM((HID, ND), BF),
            pltpu.VMEM((ND, HID), BF),
            pltpu.VMEM((ND, HID), BF),
            pltpu.VMEM((ND, HID), F32),
            pltpu.VMEM((1, 128), jnp.int32),
            pltpu.SMEM((1, 128), jnp.int32),
            pltpu.VMEM((2, 2, 128, 8, 256), BF),
            pltpu.VMEM((2, 2, 128, 8, 256), BF),
            dma((6, 2)), dma, dma((4,)), dma((3, 2)), dma((3, 2)), dma((2, 2)), dma((2, 2, 4)),
        ],
        compiler_params=pltpu.CompilerParams(
            collective_id=0, has_side_effects=True, vmem_limit_bytes=48 * 2**20
        ),
    )(
        keep(features.T), keep(weights1), keep(bias1.reshape(1, HID)), keep(weights2), keep(bias2.reshape(1, HID)),
        keep(send_rows[0].T), keep(tile_dst), keep(tile_src), tile_count, keep(tile_vals[0]),
    )


def solution(mesh):
    return jax.shard_map(
        shards,
        mesh=mesh,
        in_specs=(
            P("dp", "mp"),
            P("mp", None),
            P(),
            P(),
            P(),
            P(("dp", "mp"), None, None),
            P(("dp", "mp"), None),
            P(("dp", "mp"), None),
            P(("dp", "mp")),
            P(("dp", "mp"), None, None, None),
        ),
        out_specs=P(("dp", "mp"), None),
        check_vma=False,
    )
```
